1024 devices in a mesh: row: 32 (over x_lo, y), col: 32 (over x_hi, z, core).
Axes of the slice: x: 8 (x_hi: 2, x_lo: 4; x = x_hi * 4 + x_lo), y: 8, z: 8, core: 2. Of those that a mesh axis runs over, the one named last changes fastest.
Arguments:
- inputs: bfloat16 [128, 12288], P('col', 'row'), may hold values from -6 to 6
- w_in: bfloat16 [12288, 24576], P('row', 'col'), may hold values from -0.0546875 to 0.0546875
- w_out: bfloat16 [24576, 12288], P('col', 'row'), may hold values from -0.0390625 to 0.0390625
- grad_out: bfloat16 [128, 12288], P('col', 'row'), may hold values from -1.5 to 1.5
Outputs:
- grad_in: bfloat16 [128, 12288], P('col', 'row')
- grad_w_in: bfloat16 [12288, 24576], P('row', 'col')
- grad_w_out: bfloat16 [24576, 12288], P('col', 'row')
The draws below stay inside these ranges and needn't reach their ends.
All inputs are finite; a program needn't handle non-finite values.
Results may differ from the reference program's by a relative error of at most 0.005.
Values may be sent and summed in bfloat16 or wider, within the bound.
A program may use at most 32 MiB of HBM per device.

```python
import jax
import jax.numpy as jnp
from jax import lax

D = 12288
FF = 24576
TOKENS = 128


def steps_of(key, shape, split, low, top_value):
    loudness = 1.0
    for axis_at, shards_of in split:
        heights = jax.random.uniform(jax.random.fold_in(jax.random.fold_in(key, 6), axis_at), (shards_of,), jnp.float32, low / len(split), top_value / len(split))
        loudness = loudness * jnp.repeat(jnp.exp(heights), shape[axis_at] // shards_of).reshape((-1,) + (1,) * (len(shape) - 1 - axis_at))
    return loudness


def noise(key, dims, spread, bound, split=(), held_as=jnp.bfloat16):
    values = jax.random.normal(key, dims, jnp.float32) * spread
    if len(split) > 0:
        values = steps_of(key, dims, split, -0.22, 0.18) * values
    return jnp.clip(values, min=-bound, max=bound).astype(held_as)


def setup_inputs(seed: int = 0) -> dict:
    streams_of = jax.random.split(jax.random.key(seed), 5)
    inputs = noise(streams_of[0], (TOKENS, D), 1.0, 6.0, ((0, 32), (1, 32)))
    w_in = noise(streams_of[1], (D, FF), D ** -0.5, 0.0546875, ((0, 32), (1, 32)))
    w_out = noise(streams_of[2], (FF, D), FF ** -0.5, 0.0390625, ((0, 32), (1, 32)))
    grad_out = noise(streams_of[3], (TOKENS, D), 0.25, 1.5, ((0, 32), (1, 32)))
    return dict(inputs=inputs, w_in=w_in, w_out=w_out, grad_out=grad_out)


def gelu_pair(hidden):
    inner = 0.7978845608 * (hidden + 0.044715 * hidden * hidden * hidden)
    tvalue = jnp.tanh(inner)
    value = 0.5 * hidden * (1.0 + tvalue)
    slope = 0.5 * (1.0 + tvalue) + 0.5 * hidden * (1.0 - tvalue * tvalue) * 0.7978845608 * (1.0 + 3.0 * 0.044715 * hidden * hidden)
    return value, slope


def reference(inputs, w_in, w_out, grad_out):
    pre = jnp.dot(inputs, w_in, preferred_element_type=jnp.float32)
    value, slope = gelu_pair(pre)
    acts = value.astype(jnp.bfloat16)
    dgate = lax.dot_general(grad_out, w_out, (((1,), (1,)), ((), ())), preferred_element_type=jnp.float32)
    delta = (dgate * slope).astype(jnp.bfloat16)
    grad_w_out = lax.dot_general(acts, grad_out, (((0,), (0,)), ((), ())), preferred_element_type=jnp.float32).astype(jnp.bfloat16)
    grad_w_in = lax.dot_general(inputs, delta, (((0,), (0,)), ((), ())), preferred_element_type=jnp.float32).astype(jnp.bfloat16)
    grad_in = lax.dot_general(delta, w_in, (((1,), (1,)), ((), ())), preferred_element_type=jnp.float32).astype(jnp.bfloat16)
    return grad_in, grad_w_in, grad_w_out
```

```python
import itertools

import jax
import jax.numpy as jnp
from jax import lax
from jax.experimental import pallas as pl
from jax.experimental.pallas import tpu as pltpu
from jax.sharding import PartitionSpec as P

MESH = pl.DeviceIdType.MESH
BF16, F32 = jnp.bfloat16, jnp.float32
SIZES = dict(x_lo=4, y=8, x_hi=2, z=8, core=2)
ROWS, COLS = 32, 32
SLAB = 4
TOKENS = 128
WIDTH, HIDDEN = 384, 768
HALF = HIDDEN // 2
GROUPS = TOKENS // 8


def coordinates():
    row, col = lax.axis_index("row"), lax.axis_index("col")
    return dict(x_lo=row // 8, y=row % 8, x_hi=col // 16, z=(col // 2) % 8, core=col % 2)


def moved(me, **offsets):
    at = dict(me)
    for axis, offset in offsets.items():
        at[axis] = lax.rem(me[axis] + offset, SIZES[axis])
    return at


def device(at):
    return (at["x_lo"] * 8 + at["y"], at["x_hi"] * 16 + at["z"] * 2 + at["core"])


def shard_of(at):
    return at["x_lo"] * 8 + at["y"]


def gelu_value(hidden, tvalue):
    return 0.5 * hidden * (1.0 + tvalue)


def gelu_slope(hidden, tvalue):
    return 0.5 * (1.0 + tvalue) + 0.5 * hidden * (1.0 - tvalue * tvalue) * 0.7978845608 * (
        1.0 + 3.0 * 0.044715 * hidden * hidden
    )


def send(src, dst, send_sem, recv_sem, to):
    pltpu.make_async_remote_copy(
        src_ref=src, dst_ref=dst, send_sem=send_sem, recv_sem=recv_sem,
        device_id=to, device_id_type=MESH,
    ).start()


def drain(ref, sem):
    pltpu.make_async_copy(ref, ref, sem).wait()


def kernel(
    x_hbm, w_in_hbm, w_out_hbm, dy_hbm,
    gi_ref, gwi_ref, gwo_ref,
    x_raw, dy_raw, w_in, w_out, panels, part_out, part_in, hidden_grads, pair_out, pair_in, gi_out, gi_in,
    local_sems, send_sems, recv_sems,
):
    me = coordinates()
    shard, core, z = shard_of(me), me["core"], me["z"]
    sibling = moved(me, core=1)
    near = [moved(me, z=j) for j in (4, 3, 5, 2, 6, 1, 7)]
    far = [moved(me, x_hi=1, z=j) for j in (4, 3, 5, 2, 6, 1, 7, 0)]
    row_peers = [
        moved(me, x_lo=i, y=j)
        for i, j in sorted(itertools.product(range(4), range(8)), key=lambda o: -min(o[1], 8 - o[1]) - o[0])
        if (i, j) != (0, 0)
    ]
    upper = lax.broadcasted_iota(jnp.int32, (1, 8, 1), 1) < SLAB
    upper_rows = lax.broadcasted_iota(jnp.int32, (TOKENS, 1), 0) % 8 < SLAB
    pending = []

    loads = [
        pltpu.make_async_copy(x_hbm, x_raw, local_sems.at[0]),
        pltpu.make_async_copy(dy_hbm, dy_raw, local_sems.at[1]),
        pltpu.make_async_copy(w_in_hbm, w_in, local_sems.at[2]),
        pltpu.make_async_copy(w_out_hbm, w_out, local_sems.at[3]),
    ]
    for load in loads:
        load.start()

    barrier = pltpu.get_barrier_semaphore()
    for to in [*far, *near, *row_peers, sibling]:
        pl.semaphore_signal(barrier, inc=1, device_id=device(to), device_id_type=MESH)
    loads[0].wait()
    loads[1].wait()
    panels[0, core, z] = jnp.concatenate([x_raw[...].astype(F32), dy_raw[...].astype(F32)], axis=0).astype(BF16)
    pl.semaphore_wait(barrier, len(far) + len(near) + len(row_peers) + 1)

    own = panels.at[0, core, z]
    for to in far:
        send(own, panels.at[1, core, z], send_sems.at[10], recv_sems.at[1], device(to))
    for to in near:
        send(own, own, send_sems.at[0], recv_sems.at[0], device(to))
    pending.append((panels.at[1, 0], send_sems.at[10]))
    pending.append((panels.at[0, 0, pl.ds(0, 7)], send_sems.at[0]))

    def partial_sums(chunk):
        rows = panels.at[chunk, core]
        drain(rows if chunk else panels.at[0, core, pl.ds(0, 7)], recv_sems.at[chunk])
        send(rows, rows, send_sems.at[1 + chunk], recv_sems.at[2 + chunk], device(sibling))
        pending.append((rows, send_sems.at[1 + chunk]))
        drain(rows, recv_sems.at[2 + chunk])
        if chunk == 0:
            loads[2].wait()
            loads[3].wait()
        stacked = panels[chunk].reshape(TOKENS, WIDTH)
        pre = jnp.dot(stacked, w_in[...], preferred_element_type=F32)
        dgate = lax.dot_general(stacked, w_out[...], (((1,), (1,)), ((), ())), preferred_element_type=F32)
        both = jnp.where(upper_rows, pre, dgate)
        for h in range(2):
            part_out[chunk, pl.ds(h * GROUPS, GROUPS)] = (
                both[:, h * HALF : (h + 1) * HALF].reshape(GROUPS, 8, HALF).astype(BF16)
            )
        for to in row_peers:
            send(
                part_out.at[chunk, shard_of(to)], part_in.at[chunk, shard],
                send_sems.at[3 + chunk], recv_sems.at[4 + chunk], device(to),
            )
        part_in[chunk, shard] = part_out[chunk, shard]
        pending.append((part_in.at[chunk, pl.ds(0, 31)], send_sems.at[3 + chunk]))

    def activate(chunk):
        drain(part_in.at[chunk, pl.ds(0, 31)], recv_sems.at[4 + chunk])
        total = jnp.sum(part_in[chunk].astype(F32), axis=0)
        tvalue = jnp.tanh(0.7978845608 * (total + 0.044715 * total * total * total))
        slope = pltpu.roll(gelu_slope(total, tvalue), SLAB, 0)
        hidden_grads[chunk, shard] = jnp.where(upper[0], gelu_value(total, tvalue), total * slope).astype(BF16)
        for to in row_peers:
            mine = hidden_grads.at[chunk, shard]
            send(mine, mine, send_sems.at[5 + chunk], recv_sems.at[6 + chunk], device(to))
        pending.append((hidden_grads.at[chunk, pl.ds(0, 31)], send_sems.at[5 + chunk]))

    def half_of(chunk, h):
        return hidden_grads[chunk, pl.ds(h * GROUPS, GROUPS)].reshape(TOKENS, HALF)

    def input_grads(chunk):
        drain(hidden_grads.at[chunk, pl.ds(0, 31)], recv_sems.at[6 + chunk])
        gi = sum(
            lax.dot_general(
                half_of(chunk, h), w_in[:, h * HALF : (h + 1) * HALF],
                (((1,), (1,)), ((), ())), preferred_element_type=F32,
            )
            for h in range(2)
        ).reshape(2, 8, 8, WIDTH)
        ours = jnp.where(core == 0, gi[0], gi[1])
        pair_out[chunk] = jnp.where(core == 0, gi[1], gi[0])
        send(pair_out.at[chunk], pair_in.at[chunk], send_sems.at[7 + chunk], recv_sems.at[8 + chunk], device(sibling))
        pending.append((pair_in.at[chunk], send_sems.at[7 + chunk]))
        drain(pair_in.at[chunk], recv_sems.at[8 + chunk])
        ours = ours + pair_in[chunk]
        high = ours.astype(BF16).astype(F32)
        low = pltpu.roll(ours - high, SLAB, 1)
        gi_out[chunk] = jnp.where(upper, low, high).astype(BF16)
        for to in far if chunk else near:
            send(
                gi_out.at[chunk, to["z"]], gi_in.at[chunk, z],
                send_sems.at[11 if chunk else 9], recv_sems.at[10 + chunk], device(to),
            )
        if chunk == 0:
            gi_in[0, z] = gi_out[0, z]

    partial_sums(0)
    partial_sums(1)
    activate(0)
    activate(1)
    input_grads(0)
    input_grads(1)

    wide = panels[...].astype(F32).reshape(2, GROUPS, 8, WIDTH)
    swapped = pltpu.roll(wide.reshape(2 * GROUPS, 8, WIDTH), SLAB, 1)
    grads_out = swapped.reshape(2 * TOKENS, WIDTH).astype(BF16)
    only_inputs = jnp.where(upper, 0.0, swapped).reshape(2 * TOKENS, WIDTH).astype(BF16)
    for h in range(2):
        both = jnp.concatenate([half_of(chunk, h) for chunk in range(2)], axis=0)
        only_acts = jnp.where(upper, both.astype(F32).reshape(2 * GROUPS, 8, HALF), 0.0)
        gwo_ref[pl.ds(h * HALF, HALF), :] = lax.dot_general(
            only_acts.reshape(2 * TOKENS, HALF).astype(BF16), grads_out,
            (((0,), (0,)), ((), ())), preferred_element_type=F32,
        ).astype(BF16)
        gwi_ref[:, pl.ds(h * HALF, HALF)] = lax.dot_general(
            only_inputs, both, (((0,), (0,)), ((), ())), preferred_element_type=F32
        ).astype(BF16)

    drain(gi_in.at[0, pl.ds(0, 7)], recv_sems.at[10])
    drain(gi_in.at[1], recv_sems.at[11])
    total = jnp.sum(gi_in[...].astype(F32).reshape(16, 8, WIDTH), axis=0)
    gi_ref[...] = (total[:SLAB] + total[SLAB:]).astype(BF16)

    pending.append((gi_in.at[0, pl.ds(0, 7)], send_sems.at[9]))
    pending.append((gi_in.at[1], send_sems.at[11]))
    for copy in pending:
        drain(*copy)


def write_out(gi, gwi, gwo, gi_hbm, gwi_hbm, gwo_hbm, sems):
    copies = [
        pltpu.make_async_copy(gi, gi_hbm, sems.at[0]),
        pltpu.make_async_copy(gwi, gwi_hbm, sems.at[1]),
        pltpu.make_async_copy(gwo, gwo_hbm, sems.at[2]),
    ]
    for copy in copies:
        copy.start()
    for copy in copies:
        copy.wait()


def local(inputs, w_in, w_out, grad_out):
    hbm = pl.BlockSpec(memory_space=pltpu.HBM)
    vmem = pl.BlockSpec(memory_space=pltpu.VMEM)
    outs = pl.pallas_call(
        kernel,
        out_shape=(
            jax.ShapeDtypeStruct((SLAB, WIDTH), BF16),
            jax.ShapeDtypeStruct((WIDTH, HIDDEN), BF16),
            jax.ShapeDtypeStruct((HIDDEN, WIDTH), BF16),
        ),
        in_specs=[hbm] * 4,
        out_specs=(vmem, vmem, vmem),
        scratch_shapes=[
            pltpu.VMEM((SLAB, WIDTH), BF16),
            pltpu.VMEM((SLAB, WIDTH), BF16),
            pltpu.VMEM((WIDTH, HIDDEN), BF16),
            pltpu.VMEM((HIDDEN, WIDTH), BF16),
            pltpu.VMEM((2, 2, 8, 8, WIDTH), BF16),
            pltpu.VMEM((2, ROWS, 8, HALF), BF16),
            pltpu.VMEM((2, ROWS, 8, HALF), BF16),
            pltpu.VMEM((2, ROWS, 8, HALF), BF16),
            pltpu.VMEM((2, 8, 8, WIDTH), F32),
            pltpu.VMEM((2, 8, 8, WIDTH), F32),
            pltpu.VMEM((2, 8, 8, WIDTH), BF16),
            pltpu.VMEM((2, 8, 8, WIDTH), BF16),
            pltpu.SemaphoreType.DMA((4,)),
            pltpu.SemaphoreType.DMA((12,)),
            pltpu.SemaphoreType.DMA((12,)),
        ],
        compiler_params=pltpu.CompilerParams(
            collective_id=0, has_side_effects=True, vmem_limit_bytes=62 * 2**20
        ),
        name="ffn_backward",
    )(inputs, w_in, w_out, grad_out)
    return pl.pallas_call(
        write_out,
        out_shape=tuple(jax.ShapeDtypeStruct(out.shape, out.dtype) for out in outs),
        in_specs=[vmem] * 3,
        out_specs=(hbm, hbm, hbm),
        scratch_shapes=[pltpu.SemaphoreType.DMA((3,))],
        name="write_out",
    )(*outs)


def solution(mesh):
    return jax.shard_map(
        local,
        mesh=mesh,
        in_specs=(P("col", "row"), P("row", "col"), P("col", "row"), P("col", "row")),
        out_specs=(P("col", "row"), P("row", "col"), P("col", "row")),
        check_vma=False,
    )
```

```python
import itertools

import jax
import jax.numpy as jnp
from jax import lax
from jax.experimental import pallas as pl
from jax.experimental.pallas import tpu as pltpu
from jax.sharding import PartitionSpec as P

MESH = pl.DeviceIdType.MESH
BF16, F32 = jnp.bfloat16, jnp.float32
SIZES = dict(x_lo=4, y=8, x_hi=2, z=8, core=2)
ROWS, COLS = 32, 32
SLAB = 4
TOKENS = 128
WIDTH, HIDDEN = 384, 768
HALF = HIDDEN // 2
GROUPS = TOKENS // 8
PIECES = 4


def coordinates():
    row, col = lax.axis_index("row"), lax.axis_index("col")
    return dict(x_lo=row // 8, y=row % 8, x_hi=col // 16, z=(col // 2) % 8, core=col % 2)


def moved(me, **offsets):
    at = dict(me)
    for axis, offset in offsets.items():
        at[axis] = lax.rem(me[axis] + offset, SIZES[axis])
    return at


def device(at):
    return (at["x_lo"] * 8 + at["y"], at["x_hi"] * 16 + at["z"] * 2 + at["core"])


def shard_of(at):
    return at["x_lo"] * 8 + at["y"]


def gelu_value(hidden, tvalue):
    return 0.5 * hidden * (1.0 + tvalue)


def gelu_slope(hidden, tvalue):
    return 0.5 * (1.0 + tvalue) + 0.5 * hidden * (1.0 - tvalue * tvalue) * 0.7978845608 * (
        1.0 + 3.0 * 0.044715 * hidden * hidden
    )


def send(src, dst, send_sem, recv_sem, to):
    pltpu.make_async_remote_copy(
        src_ref=src, dst_ref=dst, send_sem=send_sem, recv_sem=recv_sem,
        device_id=to, device_id_type=MESH,
    ).start()


def drain(ref, sem):
    pltpu.make_async_copy(ref, ref, sem).wait()


def kernel(
    x_hbm, w_in_hbm, w_out_hbm, dy_hbm,
    gi_ref, gwi_hbm, gwo_hbm,
    gwi_ref, gwo_ref, x_raw, dy_raw, w_in, w_out, panels, part_out, part_in, hidden_grads, gi_out, gi_in,
    local_sems, send_sems, recv_sems, relay,
):
    me = coordinates()
    shard, core, z = shard_of(me), me["core"], me["z"]
    sibling = moved(me, core=1)
    near = [moved(me, z=j) for j in (4, 3, 5, 2, 6, 1, 7)]
    far = [moved(me, x_hi=1, z=j) for j in (4, 3, 5, 2, 6, 1, 7, 0)]
    row_peers = [
        moved(me, x_lo=i, y=j)
        for i, j in sorted(itertools.product(range(4), range(8)), key=lambda o: -min(o[1], 8 - o[1]) - o[0])
        if (i, j) != (0, 0)
    ]
    upper = lax.broadcasted_iota(jnp.int32, (1, 8, 1), 1) < SLAB
    upper_rows = lax.broadcasted_iota(jnp.int32, (TOKENS, 1), 0) % 8 < SLAB
    pending = []

    loads = [
        pltpu.make_async_copy(x_hbm, x_raw, local_sems.at[0]),
        pltpu.make_async_copy(dy_hbm, dy_raw, local_sems.at[1]),
        pltpu.make_async_copy(w_in_hbm, w_in, local_sems.at[2]),
        pltpu.make_async_copy(w_out_hbm, w_out, local_sems.at[3]),
    ]
    for load in loads:
        load.start()

    lines = [moved(me, y=j) for j in (4, 3, 5, 2, 6, 1, 7)]
    greeted = [*far, *near, *lines, *[moved(me, x_lo=i) for i in (3, 2, 1)], sibling]
    barrier = pltpu.get_barrier_semaphore()
    for to in greeted:
        pl.semaphore_signal(barrier, inc=1, device_id=device(to), device_id_type=MESH)
    loads[0].wait()
    loads[1].wait()
    panels[0, core, z] = jnp.concatenate([x_raw[...].astype(F32), dy_raw[...].astype(F32)], axis=0).astype(BF16)
    pl.semaphore_wait(barrier, len(greeted))

    own = panels.at[0, core, z]
    for to in far:
        send(own, panels.at[1, core, z], send_sems.at[10], recv_sems.at[1], device(to))
    for to in near:
        send(own, own, send_sems.at[0], recv_sems.at[0], device(to))
    for to in lines:
        pl.semaphore_signal(relay, inc=1, device_id=device(to), device_id_type=MESH)
    pending.append((panels.at[1, 0], send_sems.at[10]))
    pending.append((panels.at[0, 0, pl.ds(0, 7)], send_sems.at[0]))

    def partial_sums(chunk):
        rows = panels.at[chunk, core]
        drain(rows if chunk else panels.at[0, core, pl.ds(0, 7)], recv_sems.at[chunk])
        send(rows, rows, send_sems.at[1 + chunk], recv_sems.at[2 + chunk], device(sibling))
        pending.append((rows, send_sems.at[1 + chunk]))
        drain(rows, recv_sems.at[2 + chunk])
        if chunk == 0:
            loads[2].wait()
            loads[3].wait()
            pl.semaphore_wait(relay, len(lines))
        stacked = panels[chunk].reshape(TOKENS, WIDTH)
        pre = jnp.dot(stacked, w_in[...], preferred_element_type=F32)
        dgate = lax.dot_general(stacked, w_out[...], (((1,), (1,)), ((), ())), preferred_element_type=F32)
        both = jnp.where(upper_rows, pre, dgate)
        for h in range(2):
            part_out[chunk, pl.ds(h * GROUPS, GROUPS)] = (
                both[:, h * HALF : (h + 1) * HALF].reshape(GROUPS, 8, HALF).astype(BF16)
            )
        for to in row_peers:
            send(
                part_out.at[chunk, shard_of(to)], part_in.at[chunk, shard],
                send_sems.at[3 + chunk], recv_sems.at[4 + chunk], device(to),
            )
        part_in[chunk, shard] = part_out[chunk, shard]
        pending.append((part_in.at[chunk, pl.ds(0, 31)], send_sems.at[3 + chunk]))

    def activate(chunk):
        drain(part_in.at[chunk, pl.ds(0, 31)], recv_sems.at[4 + chunk])
        total = jnp.sum(part_in[chunk].astype(F32), axis=0)
        tvalue = jnp.tanh(0.7978845608 * (total + 0.044715 * total * total * total))
        slope = pltpu.roll(gelu_slope(total, tvalue), SLAB, 0)
        hidden_grads[chunk, shard] = jnp.where(upper[0], gelu_value(total, tvalue), total * slope).astype(BF16)
        for to in row_peers:
            mine = hidden_grads.at[chunk, shard]
            send(mine, mine, send_sems.at[5 + chunk], recv_sems.at[6 + chunk], device(to))
        pending.append((hidden_grads.at[chunk, pl.ds(0, 31)], send_sems.at[5 + chunk]))

    def half_of(chunk, h):
        return hidden_grads[chunk, pl.ds(h * GROUPS, GROUPS)].reshape(TOKENS, HALF)

    def input_grads(chunk):
        drain(hidden_grads.at[chunk, pl.ds(0, 31)], recv_sems.at[6 + chunk])
        gi = sum(
            lax.dot_general(
                half_of(chunk, h), w_in[:, h * HALF : (h + 1) * HALF],
                (((1,), (1,)), ((), ())), preferred_element_type=F32,
            )
            for h in range(2)
        ).reshape(GROUPS, 8, WIDTH)
        gi_out[chunk] = gi[:, SLAB:].astype(BF16)
        there = far if chunk else near
        both = [*there, *[moved(to, core=1) for to in there], *([] if chunk else [sibling])]
        for to in both:
            send(
                gi_out.at[chunk, to["core"] * 8 + to["z"]], gi_in.at[chunk, core * 8 + z],
                send_sems.at[7 + chunk], recv_sems.at[8 + chunk], device(to),
            )
        if chunk == 0:
            gi_in[0, core * 8 + z] = gi_out[0, core * 8 + z]

    partial_sums(0)
    partial_sums(1)
    activate(0)
    activate(1)
    input_grads(0)
    input_grads(1)

    wide = panels[...].astype(F32).reshape(2, GROUPS, 8, WIDTH)
    swapped = pltpu.roll(wide.reshape(2 * GROUPS, 8, WIDTH), SLAB, 1)
    grads_out = swapped.reshape(2 * TOKENS, WIDTH).astype(BF16)
    only_inputs = jnp.where(upper, 0.0, swapped).reshape(2 * TOKENS, WIDTH).astype(BF16)
    for h in range(2):
        both = jnp.concatenate([half_of(chunk, h) for chunk in range(2)], axis=0)
        only_acts = jnp.where(upper, both.astype(F32).reshape(2 * GROUPS, 8, HALF), 0.0)
        gwo_ref[pl.ds(h * HALF, HALF), :] = lax.dot_general(
            only_acts.reshape(2 * TOKENS, HALF).astype(BF16), grads_out,
            (((0,), (0,)), ((), ())), preferred_element_type=F32,
        ).astype(BF16)
        gwi_ref[:, pl.ds(h * HALF, HALF)] = lax.dot_general(
            only_inputs, both, (((0,), (0,)), ((), ())), preferred_element_type=F32
        ).astype(BF16)

    stores = [
        pltpu.make_async_copy(gwi_ref, gwi_hbm, local_sems.at[4]),
        pltpu.make_async_copy(gwo_ref, gwo_hbm, local_sems.at[5]),
    ]
    for store in stores:
        store.start()
    nearby, distant = gi_in.at[0, pl.ds(0, 15)], gi_in.at[1]
    drain(nearby, recv_sems.at[8])
    drain(distant, recv_sems.at[9])
    gi_ref[...] = jnp.sum(gi_in[...].astype(F32).reshape(32, SLAB, WIDTH), axis=0).astype(BF16)

    pending.append((nearby, send_sems.at[7]))
    pending.append((distant, send_sems.at[8]))
    for store in stores:
        store.wait()
    for copy in pending:
        drain(*copy)


def write_out(gi, gwi, gwo, gi_hbm, gwi_hbm, gwo_hbm, gi_vmem, gwi_vmem, gwo_vmem, in_sems, out_sems):
    loads, stores = [], []

    def through(source, held, target, pieces):
        rows = source.shape[0] // pieces
        for piece in range(pieces):
            part, at = pl.ds(piece * rows, rows), len(loads)
            loads.append(pltpu.make_async_copy(source.at[part], held.at[part], in_sems.at[at]))
            stores.append(pltpu.make_async_copy(held.at[part], target.at[part], out_sems.at[at]))

    through(gwi, gwi_vmem, gwi_hbm, PIECES)
    through(gwo, gwo_vmem, gwo_hbm, PIECES)
    through(gi, gi_vmem, gi_hbm, 1)
    for load in loads:
        load.start()
    for load, store in zip(loads, stores):
        load.wait()
        store.start()
    for store in stores:
        store.wait()


def local(inputs, w_in, w_out, grad_out):
    hbm = pl.BlockSpec(memory_space=pltpu.HBM)
    vmem = pl.BlockSpec(memory_space=pltpu.VMEM)
    outs = pl.pallas_call(
        kernel,
        out_shape=(
            jax.ShapeDtypeStruct((SLAB, WIDTH), BF16),
            jax.ShapeDtypeStruct((WIDTH, HIDDEN), BF16),
            jax.ShapeDtypeStruct((HIDDEN, WIDTH), BF16),
        ),
        in_specs=[hbm] * 4,
        out_specs=(vmem, hbm, hbm),
        scratch_shapes=[
            pltpu.VMEM((WIDTH, HIDDEN), BF16),
            pltpu.VMEM((HIDDEN, WIDTH), BF16),
            pltpu.VMEM((SLAB, WIDTH), BF16),
            pltpu.VMEM((SLAB, WIDTH), BF16),
            pltpu.VMEM((WIDTH, HIDDEN), BF16),
            pltpu.VMEM((HIDDEN, WIDTH), BF16),
            pltpu.VMEM((2, 2, 8, 8, WIDTH), BF16),
            pltpu.VMEM((2, ROWS, 8, HALF), BF16),
            pltpu.VMEM((2, ROWS, 8, HALF), BF16),
            pltpu.VMEM((2, ROWS, 8, HALF), BF16),
            pltpu.VMEM((2, GROUPS, SLAB, WIDTH), BF16),
            pltpu.VMEM((2, GROUPS, SLAB, WIDTH), BF16),
            pltpu.SemaphoreType.DMA((6,)),
            pltpu.SemaphoreType.DMA((12,)),
            pltpu.SemaphoreType.DMA((12,)),
            pltpu.SemaphoreType.REGULAR,
        ],
        compiler_params=pltpu.CompilerParams(
            collective_id=0, has_side_effects=True, vmem_limit_bytes=62 * 2**20
        ),
        name="ffn_backward",
    )(inputs, w_in, w_out, grad_out)
    return pl.pallas_call(
        write_out,
        out_shape=tuple(jax.ShapeDtypeStruct(out.shape, out.dtype) for out in outs),
        in_specs=[hbm, hbm, hbm],
        out_specs=(hbm, hbm, hbm),
        scratch_shapes=[
            *[pltpu.VMEM(out.shape, out.dtype) for out in outs],
            pltpu.SemaphoreType.DMA((1 + 2 * PIECES,)),
            pltpu.SemaphoreType.DMA((1 + 2 * PIECES,)),
        ],
        name="write_out",
    )(*outs)


def solution(mesh):
    return jax.shard_map(
        local,
        mesh=mesh,
        in_specs=(P("col", "row"), P("row", "col"), P("col", "row"), P("col", "row")),
        out_specs=(P("col", "row"), P("row", "col"), P("col", "row")),
        check_vma=False,
    )
```

```python
import itertools

import jax
import jax.numpy as jnp
from jax import lax
from jax.experimental import pallas as pl
from jax.experimental.pallas import tpu as pltpu
from jax.sharding import PartitionSpec as P

MESH = pl.DeviceIdType.MESH
BF16, F32 = jnp.bfloat16, jnp.float32
SIZES = dict(x_lo=4, y=8, x_hi=2, z=8, core=2)
ROWS, COLS = 32, 32
SLAB = 4
TOKENS = 128
WIDTH, HIDDEN = 384, 768
HALF = HIDDEN // 2
GROUPS = TOKENS // 8
PIECES = 4


def coordinates():
    row, col = lax.axis_index("row"), lax.axis_index("col")
    return dict(x_lo=row // 8, y=row % 8, x_hi=col // 16, z=(col // 2) % 8, core=col % 2)


def moved(me, **offsets):
    at = dict(me)
    for axis, offset in offsets.items():
        at[axis] = lax.rem(me[axis] + offset, SIZES[axis])
    return at


def device(at):
    return (at["x_lo"] * 8 + at["y"], at["x_hi"] * 16 + at["z"] * 2 + at["core"])


def shard_of(at):
    return at["x_lo"] * 8 + at["y"]


def gelu_value(hidden, tvalue):
    return 0.5 * hidden * (1.0 + tvalue)


def gelu_slope(hidden, tvalue):
    return 0.5 * (1.0 + tvalue) + 0.5 * hidden * (1.0 - tvalue * tvalue) * 0.7978845608 * (
        1.0 + 3.0 * 0.044715 * hidden * hidden
    )


def send(src, dst, send_sem, recv_sem, to):
    pltpu.make_async_remote_copy(
        src_ref=src, dst_ref=dst, send_sem=send_sem, recv_sem=recv_sem,
        device_id=to, device_id_type=MESH,
    ).start()


def drain(ref, sem):
    pltpu.make_async_copy(ref, ref, sem).wait()


def kernel(
    x_hbm, w_in_hbm, w_out_hbm, dy_hbm,
    gi_in, gwi_hbm, gwo_hbm,
    gwi_ref, gwo_ref, x_raw, dy_raw, w_in, w_out, panels, part_out, part_in, hidden_grads, gi_out,
    local_sems, send_sems, recv_sems, relay,
):
    me = coordinates()
    shard, core, z = shard_of(me), me["core"], me["z"]
    sibling = moved(me, core=1)
    near = [moved(me, z=j) for j in (4, 3, 5, 2, 6, 1, 7)]
    far = [moved(me, x_hi=1, z=j) for j in (4, 3, 5, 2, 6, 1, 7, 0)]
    row_peers = [
        moved(me, x_lo=i, y=j)
        for i, j in sorted(itertools.product(range(4), range(8)), key=lambda o: -min(o[1], 8 - o[1]) - o[0])
        if (i, j) != (0, 0)
    ]
    upper = lax.broadcasted_iota(jnp.int32, (1, 8, 1), 1) < SLAB
    upper_rows = lax.broadcasted_iota(jnp.int32, (TOKENS, 1), 0) % 8 < SLAB
    pending, stores = [], []

    loads = [
        pltpu.make_async_copy(x_hbm, x_raw, local_sems.at[0]),
        pltpu.make_async_copy(dy_hbm, dy_raw, local_sems.at[1]),
        pltpu.make_async_copy(w_in_hbm, w_in, local_sems.at[2]),
        pltpu.make_async_copy(w_out_hbm, w_out, local_sems.at[3]),
    ]
    for load in loads:
        load.start()

    lines = [moved(me, y=j) for j in (4, 3, 5, 2, 6, 1, 7)]
    greeted = [*far, *near, *lines, *[moved(me, x_lo=i) for i in (3, 2, 1)], sibling]
    barrier = pltpu.get_barrier_semaphore()
    for to in greeted:
        pl.semaphore_signal(barrier, inc=1, device_id=device(to), device_id_type=MESH)
    loads[0].wait()
    loads[1].wait()
    panels[0, core, z] = jnp.concatenate([x_raw[...].astype(F32), dy_raw[...].astype(F32)], axis=0).astype(BF16)
    pl.semaphore_wait(barrier, len(greeted))

    own = panels.at[0, core, z]
    for to in far:
        send(own, panels.at[1, core, z], send_sems.at[10], recv_sems.at[1], device(to))
    for to in near:
        send(own, own, send_sems.at[0], recv_sems.at[0], device(to))
    for to in lines:
        pl.semaphore_signal(relay, inc=1, device_id=device(to), device_id_type=MESH)
    pending.append((panels.at[1, 0], send_sems.at[10]))
    pending.append((panels.at[0, 0, pl.ds(0, 7)], send_sems.at[0]))

    def partial_sums(chunk):
        rows = panels.at[chunk, core]
        drain(rows if chunk else panels.at[0, core, pl.ds(0, 7)], recv_sems.at[chunk])
        send(rows, rows, send_sems.at[1 + chunk], recv_sems.at[2 + chunk], device(sibling))
        pending.append((rows, send_sems.at[1 + chunk]))
        drain(rows, recv_sems.at[2 + chunk])
        if chunk == 0:
            loads[2].wait()
            loads[3].wait()
            pl.semaphore_wait(relay, len(lines))
        stacked = panels[chunk].reshape(TOKENS, WIDTH)
        pre = jnp.dot(stacked, w_in[...], preferred_element_type=F32)
        dgate = lax.dot_general(stacked, w_out[...], (((1,), (1,)), ((), ())), preferred_element_type=F32)
        both = jnp.where(upper_rows, pre, dgate)
        for h in range(2):
            part_out[chunk, pl.ds(h * GROUPS, GROUPS)] = (
                both[:, h * HALF : (h + 1) * HALF].reshape(GROUPS, 8, HALF).astype(BF16)
            )
        for to in row_peers:
            send(
                part_out.at[chunk, shard_of(to)], part_in.at[chunk, shard],
                send_sems.at[3 + chunk], recv_sems.at[4 + chunk], device(to),
            )
        part_in[chunk, shard] = part_out[chunk, shard]
        pending.append((part_in.at[chunk, pl.ds(0, 31)], send_sems.at[3 + chunk]))

    def activate(chunk):
        drain(part_in.at[chunk, pl.ds(0, 31)], recv_sems.at[4 + chunk])
        total = jnp.sum(part_in[chunk].astype(F32), axis=0)
        tvalue = jnp.tanh(0.7978845608 * (total + 0.044715 * total * total * total))
        slope = pltpu.roll(gelu_slope(total, tvalue), SLAB, 0)
        hidden_grads[chunk, shard] = jnp.where(upper[0], gelu_value(total, tvalue), total * slope).astype(BF16)
        for to in row_peers:
            mine = hidden_grads.at[chunk, shard]
            send(mine, mine, send_sems.at[5 + chunk], recv_sems.at[6 + chunk], device(to))
        pending.append((hidden_grads.at[chunk, pl.ds(0, 31)], send_sems.at[5 + chunk]))

    def half_of(chunk, h):
        return hidden_grads[chunk, pl.ds(h * GROUPS, GROUPS)].reshape(TOKENS, HALF)

    def input_grads(chunk):
        drain(hidden_grads.at[chunk, pl.ds(0, 31)], recv_sems.at[6 + chunk])
        gi = sum(
            lax.dot_general(
                half_of(chunk, h), w_in[:, h * HALF : (h + 1) * HALF],
                (((1,), (1,)), ((), ())), preferred_element_type=F32,
            )
            for h in range(2)
        ).reshape(GROUPS, 8, WIDTH)
        gi_out[chunk] = gi[:, SLAB:].astype(BF16)
        there = far if chunk else near
        both = [at for to in there for at in (to, moved(to, core=1))] + ([] if chunk else [sibling])
        for to in both:
            send(
                gi_out.at[chunk, to["core"] * 8 + to["z"]], gi_in.at[chunk, core * 8 + z],
                send_sems.at[7 + chunk], recv_sems.at[8 + chunk], device(to),
            )
        if chunk == 0:
            stores.append(pltpu.make_async_copy(
                gi_out.at[0, core * 8 + z], gi_in.at[0, core * 8 + z], local_sems.at[6]
            ))
            stores[0].start()

    partial_sums(0)
    partial_sums(1)
    activate(0)
    activate(1)
    input_grads(0)
    input_grads(1)

    wide = panels[...].astype(F32).reshape(2, GROUPS, 8, WIDTH)
    swapped = pltpu.roll(wide.reshape(2 * GROUPS, 8, WIDTH), SLAB, 1)
    grads_out = swapped.reshape(2 * TOKENS, WIDTH).astype(BF16)
    only_inputs = jnp.where(upper, 0.0, swapped).reshape(2 * TOKENS, WIDTH).astype(BF16)
    for h in range(2):
        both = jnp.concatenate([half_of(chunk, h) for chunk in range(2)], axis=0)
        only_acts = jnp.where(upper, both.astype(F32).reshape(2 * GROUPS, 8, HALF), 0.0)
        gwo_ref[pl.ds(h * HALF, HALF), :] = lax.dot_general(
            only_acts.reshape(2 * TOKENS, HALF).astype(BF16), grads_out,
            (((0,), (0,)), ((), ())), preferred_element_type=F32,
        ).astype(BF16)
        gwi_ref[:, pl.ds(h * HALF, HALF)] = lax.dot_general(
            only_inputs, both, (((0,), (0,)), ((), ())), preferred_element_type=F32
        ).astype(BF16)

    stores.append(pltpu.make_async_copy(gwi_ref, gwi_hbm, local_sems.at[4]))
    stores.append(pltpu.make_async_copy(gwo_ref, gwo_hbm, local_sems.at[5]))
    stores[1].start()
    stores[2].start()
    nearby, distant = gi_in.at[0, pl.ds(0, 15)], gi_in.at[1]
    drain(nearby, recv_sems.at[8])
    drain(distant, recv_sems.at[9])
    pending.append((nearby, send_sems.at[7]))
    pending.append((distant, send_sems.at[8]))
    for store in stores:
        store.wait()
    for copy in pending:
        drain(*copy)


def write_out(slabs, gwi, gwo, gi_hbm, gwi_hbm, gwo_hbm, held, gi_vmem, gwi_vmem, gwo_vmem, in_sems, out_sems):
    loads, stores = [], []

    def through(source, buffer, target):
        rows = source.shape[0] // PIECES
        for piece in range(PIECES):
            part, at = pl.ds(piece * rows, rows), len(loads)
            loads.append(pltpu.make_async_copy(source.at[part], buffer.at[part], in_sems.at[at]))
            stores.append(pltpu.make_async_copy(buffer.at[part], target.at[part], out_sems.at[at]))

    through(gwi, gwi_vmem, gwi_hbm)
    through(gwo, gwo_vmem, gwo_hbm)
    fetch = pltpu.make_async_copy(slabs, held, in_sems.at[2 * PIECES])
    fetch.start()
    for load in loads:
        load.start()
    fetch.wait()
    gi_vmem[...] = jnp.sum(held[...].astype(F32).reshape(32, SLAB, WIDTH), axis=0).astype(BF16)
    last = pltpu.make_async_copy(gi_vmem, gi_hbm, out_sems.at[2 * PIECES])
    last.start()
    for load, store in zip(loads, stores):
        load.wait()
        store.start()
    for store in stores:
        store.wait()
    last.wait()


def local(inputs, w_in, w_out, grad_out):
    hbm = pl.BlockSpec(memory_space=pltpu.HBM)
    vmem = pl.BlockSpec(memory_space=pltpu.VMEM)
    outs = pl.pallas_call(
        kernel,
        out_shape=(
            jax.ShapeDtypeStruct((2, GROUPS, SLAB, WIDTH), BF16),
            jax.ShapeDtypeStruct((WIDTH, HIDDEN), BF16),
            jax.ShapeDtypeStruct((HIDDEN, WIDTH), BF16),
        ),
        in_specs=[hbm] * 4,
        out_specs=(hbm, hbm, hbm),
        scratch_shapes=[
            pltpu.VMEM((WIDTH, HIDDEN), BF16),
            pltpu.VMEM((HIDDEN, WIDTH), BF16),
            pltpu.VMEM((SLAB, WIDTH), BF16),
            pltpu.VMEM((SLAB, WIDTH), BF16),
            pltpu.VMEM((WIDTH, HIDDEN), BF16),
            pltpu.VMEM((HIDDEN, WIDTH), BF16),
            pltpu.VMEM((2, 2, 8, 8, WIDTH), BF16),
            pltpu.VMEM((2, ROWS, 8, HALF), BF16),
            pltpu.VMEM((2, ROWS, 8, HALF), BF16),
            pltpu.VMEM((2, ROWS, 8, HALF), BF16),
            pltpu.VMEM((2, GROUPS, SLAB, WIDTH), BF16),
            pltpu.SemaphoreType.DMA((7,)),
            pltpu.SemaphoreType.DMA((12,)),
            pltpu.SemaphoreType.DMA((12,)),
            pltpu.SemaphoreType.REGULAR,
        ],
        compiler_params=pltpu.CompilerParams(
            collective_id=0, has_side_effects=True, vmem_limit_bytes=62 * 2**20
        ),
        name="ffn_backward",
    )(inputs, w_in, w_out, grad_out)
    return pl.pallas_call(
        write_out,
        out_shape=(
            jax.ShapeDtypeStruct((SLAB, WIDTH), BF16),
            jax.ShapeDtypeStruct((WIDTH, HIDDEN), BF16),
            jax.ShapeDtypeStruct((HIDDEN, WIDTH), BF16),
        ),
        in_specs=[hbm, hbm, hbm],
        out_specs=(hbm, hbm, hbm),
        scratch_shapes=[
            pltpu.VMEM((2, GROUPS, SLAB, WIDTH), BF16),
            pltpu.VMEM((SLAB, WIDTH), BF16),
            pltpu.VMEM((WIDTH, HIDDEN), BF16),
            pltpu.VMEM((HIDDEN, WIDTH), BF16),
            pltpu.SemaphoreType.DMA((1 + 2 * PIECES,)),
            pltpu.SemaphoreType.DMA((1 + 2 * PIECES,)),
        ],
        name="write_out",
    )(*outs)


def solution(mesh):
    return jax.shard_map(
        local,
        mesh=mesh,
        in_specs=(P("col", "row"), P("row", "col"), P("col", "row"), P("col", "row")),
        out_specs=(P("col", "row"), P("row", "col"), P("col", "row")),
        check_vma=False,
    )
```
